512 devices in a mesh: gx: 8 (over z_hi, y), gy: 8 (over x, core), gz: 8 (over z_lo).
Axes of the slice: x: 4, y: 4, z: 16 (z_hi: 2, z_lo: 8; z = z_hi * 8 + z_lo), core: 2. Of those that a mesh axis runs over, the one named last changes fastest.
Arguments:
- species: float32 [512, 512, 1024], P('gx', 'gz', 'gy'), may hold values from -6 to 6
- factor_y: float32 [1024, 96], P('gy'), may hold values from -0.1875 to 0.1875
- factor_z: float32 [512, 96], P('gz'), may hold values from -0.25 to 0.25
Outputs:
- gram: float32 [512, 512], P('gx', ('gy', 'gz'))
The draws below stay inside these ranges and needn't reach their ends.
All inputs are finite; a program needn't handle non-finite values.
Results may differ from the reference program's by a relative error of at most 0.000062.
Values sent between devices are 32-bit elements; how exact they have to be, the bound alone decides.
No kernel may reach another device: no remote copies, remote signals or barrier semaphores. Data moves between devices by JAX's collectives and lax.ppermute only.
A program may use at most 64 MiB of HBM per device.

```python
import jax
import jax.numpy as jnp
from jax import lax

R = 96
NX = 512
NY = 1024
NZ = 512


def steps_of(key, dims, cuts, smallest, largest):
    gain = 1.0
    for position, shards_of in cuts:
        steps = jax.random.uniform(jax.random.fold_in(jax.random.fold_in(key, 6), position), (shards_of,), jnp.float32, smallest / len(cuts), largest / len(cuts))
        gain = gain * jnp.repeat(jnp.exp(steps), dims[position] // shards_of).reshape((-1,) + (1,) * (len(dims) - 1 - position))
    return gain


def bell_draw(rng, dims, deviation, limit, pieces=(), kind=jnp.bfloat16):
    values = jax.random.normal(rng, dims, jnp.float32) * deviation
    if len(pieces) > 0:
        values = steps_of(rng, dims, pieces, -0.22, 0.18) * values
    return jnp.clip(values, min=-limit, max=limit).astype(kind)


def setup_inputs(seed: int = 0) -> dict:
    streams_of = jax.random.split(jax.random.key(seed), 4)
    return {
        "species": bell_draw(streams_of[0], (NX, NZ, NY), 1.0, 6.0, ((0, 8), (1, 8), (2, 8)), jnp.float32),
        "factor_y": bell_draw(streams_of[1], (NY, R), NY ** -0.5, 0.1875, ((0, 8),), jnp.float32),
        "factor_z": bell_draw(streams_of[2], (NZ, R), NZ ** -0.5, 0.25, ((0, 8),), jnp.float32),
    }


def reference(species, factor_y, factor_z):
    high = lax.Precision.HIGHEST
    partial_y = jnp.einsum("xzy,yr->xzr", species, factor_y, precision=high)
    projected = jnp.einsum("xzr,zs->xsr", partial_y, factor_z, precision=high)
    flat = projected.reshape(projected.shape[0], -1)
    gram = jnp.dot(flat, flat.T, precision=high, preferred_element_type=jnp.float32)
    return gram / (R * R)
```

```python
import jax
import jax.numpy as jnp
from jax import lax
from jax.sharding import Mesh, PartitionSpec as P

R = 96
HIGH = lax.Precision.HIGH


def body(species, factor_y, factor_z):
    y = lax.axis_index("y")
    x = lax.axis_index("x")
    c = lax.axis_index("c")
    all_z = lax.all_gather(factor_z, "g", axis=0, tiled=True)

    own = species.reshape(4, 16 * 64, 128)
    mine = lax.dynamic_slice(factor_y, (0, c * 48), (128, 48))
    others = lax.dynamic_slice(factor_y, (0, (1 - c) * 48), (128, 48))
    sent = jnp.einsum("jmy,yr->jrm", own, others, precision=HIGH)
    sent = lax.ppermute(sent, "c", [(0, 1), (1, 0)])
    along_y = jnp.einsum("jmy,yr->jrm", own, mine, precision=HIGH) + sent
    along_y = lax.all_to_all(along_y, "x", 0, 0, tiled=True).sum(0)

    parts = along_y.reshape(16, 24, 128)
    parts = lax.all_to_all(parts, ("h", "g"), 0, 0, tiled=True)
    parts = parts.reshape(2, 8, 3, 16, 64)
    both = jnp.einsum("hgixz,gzs->hixs", parts, all_z.reshape(8, 64, R), precision=HIGH)

    both = jnp.pad(both.reshape(96, R), ((0, 0), (0, 32)))
    both = lax.all_to_all(jnp.broadcast_to(both, (16, 96, 128)), ("y", "x"), 0, 0, tiled=True)
    both = both.reshape(4, 4, 2, 3, 16, 128)
    rows = lax.dynamic_index_in_dim(both, y, 0, keepdims=False)
    cols = lax.dynamic_slice(both, (2 * (x % 2), 0, x // 2, 0, 0, 0), (2, 4, 1, 3, 16, 128))[:, :, 0]
    terms = jnp.einsum("bjims,khins->bjmhkn", cols, rows, precision=HIGH)
    terms = terms.reshape(2, 8, 8, 2, 64).transpose(0, 3, 1, 2, 4).reshape(32, 4, 128)
    terms = lax.all_to_all(terms, ("c", "h", "g"), 0, 0, tiled=True).sum(0)
    return terms.reshape(8, 64).T / (R * R)


def solution(mesh):
    fine = Mesh(mesh.devices.reshape(2, 4, 4, 2, 8), ("h", "y", "x", "c", "g"))
    placed = (P(("h", "y"), "g", ("x", "c")), P(("x", "c"), None), P("g", None))
    return jax.shard_map(
        body, mesh=fine, in_specs=placed, out_specs=P(("h", "y"), ("x", "c", "g")), check_vma=False
    )
```

```python
import jax
import jax.numpy as jnp
from jax import lax
from jax.sharding import Mesh, PartitionSpec as P

R = 96
HIGH = lax.Precision.HIGH
HIGHEST = lax.Precision.HIGHEST


def body(species, factor_y, factor_z):
    y = lax.axis_index("y")
    x = lax.axis_index("x")
    c = lax.axis_index("c")
    four_z = jnp.einsum("ab,zs->azbs", jnp.eye(4, dtype=jnp.float32), factor_z).reshape(256, 384)

    own = species.reshape(4, 16 * 64, 128)
    halves = jnp.stack([
        lax.dynamic_slice(factor_y, (0, (1 - c) * 48), (128, 48)),
        lax.dynamic_slice(factor_y, (0, c * 48), (128, 48)),
    ])
    along_y = jnp.einsum("jmy,qyr->qjrm", own, halves, precision=HIGH)
    along_y = along_y[1] + lax.ppermute(along_y[0], "c", [(0, 1), (1, 0)])
    along_y = lax.all_to_all(along_y, "x", 0, 0, tiled=True).sum(0)

    parts = jnp.einsum("rta,ab->rtb", along_y.reshape(48, 4, 256), four_z, precision=HIGHEST)
    parts = parts.reshape(16, 3, 4, 3, 128).transpose(0, 1, 3, 2, 4).reshape(144, 4, 128)
    parts = lax.all_to_all(parts, ("h", "g"), 0, 0, tiled=True)
    both = parts.reshape(2, 8, 9, 4, 128).sum(1).transpose(1, 0, 2, 3).reshape(9, 8, 128)

    both = jnp.broadcast_to(both, (16, 9, 8, 128)).reshape(144, 8, 128)
    both = lax.all_to_all(both, ("y", "x"), 0, 0, tiled=True)
    both = both.reshape(4, 4, 3, 3, 2, 4, 128)
    rows = lax.dynamic_index_in_dim(both, y, 0, keepdims=False)
    cols = lax.dynamic_slice(both, (2 * (x % 2), 0, 0, 0, x // 2, 0, 0), (2, 4, 3, 3, 1, 4, 128))[:, :, :, :, 0]
    rows = rows.transpose(3, 0, 4, 1, 2, 5).reshape(2, 4, 4, 3, 4, 96)
    cols = cols.transpose(0, 1, 4, 2, 3, 5).reshape(2, 4, 4, 3, 4, 96)
    terms = jnp.einsum("cjtias,hkuibs->cjtahkub", cols, rows, precision=HIGHEST)
    terms = terms.reshape(2, 8, 8, 2, 64).transpose(0, 3, 1, 2, 4).reshape(32, 4, 128)
    terms = lax.all_to_all(terms, ("c", "h", "g"), 0, 0, tiled=True).sum(0)
    return terms.reshape(8, 64).T / (R * R)


def solution(mesh):
    fine = Mesh(mesh.devices.reshape(2, 4, 4, 2, 8), ("h", "y", "x", "c", "g"))
    placed = (P(("h", "y"), "g", ("x", "c")), P(("x", "c"), None), P("g", None))
    return jax.shard_map(
        body, mesh=fine, in_specs=placed, out_specs=P(("h", "y"), ("x", "c", "g")), check_vma=False
    )
```

```python
import jax
import jax.numpy as jnp
from jax import lax
from jax.experimental import pallas as pl
from jax.experimental.pallas import tpu as pltpu
from jax.sharding import Mesh, PartitionSpec as P

R = 96
HIGHEST = lax.Precision.HIGHEST
F32 = jnp.float32
BF16 = jnp.bfloat16
PARAMS = pltpu.CompilerParams(vmem_limit_bytes=32 * 1024 * 1024)


def split(value):
    top = value.astype(BF16)
    return top, (value - top.astype(F32)).astype(BF16)


def dot_nt(left, right):
    return lax.dot_general(left, right, (((1,), (1,)), ((), ())), preferred_element_type=F32)


def y_kernel(species_hbm, factor_hbm, others_ref, mine_ref, field_ref, factor_ref, left_ref, sems):
    c = lax.axis_index("c")
    copies = [pltpu.make_async_copy(factor_hbm, factor_ref, sems.at[4])]
    for j in range(4):
        rows = pl.ds(16 * j, 16)
        copies.append(pltpu.make_async_copy(species_hbm.at[rows], field_ref.at[rows], sems.at[j]))
    for copy in copies:
        copy.start()
    copies[0].wait()
    top, low = split(factor_ref[...])
    left_ref[0:R, 0:128] = top
    left_ref[0:R, 128:256] = top
    left_ref[R:192, 0:128] = low
    left_ref[R:192, 128:256] = jnp.zeros_like(low)
    for j in range(4):
        copies[1 + j].wait()
        top, low = split(field_ref[16 * j : 16 * j + 16].reshape(1024, 128))
        both = dot_nt(left_ref[...], jnp.concatenate([top, low], axis=1))
        both = both[0:R] + both[R:192]

        @pl.when(c == 0)
        def _():
            mine_ref[j] = both[0:48]
            others_ref[j] = both[48:96]

        @pl.when(c == 1)
        def _():
            others_ref[j] = both[0:48]
            mine_ref[j] = both[48:96]


def y_product(species, factor_y):
    half = jax.ShapeDtypeStruct((4, 48, 1024), F32)
    hbm = pl.BlockSpec(memory_space=pltpu.HBM)
    return pl.pallas_call(
        y_kernel,
        in_specs=[hbm, hbm],
        out_shape=[half, half],
        scratch_shapes=[
            pltpu.VMEM((64, 64, 128), F32),
            pltpu.VMEM((R, 128), F32),
            pltpu.VMEM((192, 256), BF16),
            pltpu.SemaphoreType.DMA((5,)),
        ],
        compiler_params=PARAMS,
    )(pltpu.with_memory_space_constraint(species, pltpu.HBM), pltpu.with_memory_space_constraint(factor_y.T, pltpu.HBM))


def add_kernel(a_ref, b_ref, out_ref):
    out_ref[...] = a_ref[...] + b_ref[...]


def add(a, b):
    return pl.pallas_call(
        add_kernel, out_shape=pltpu.VMEM(a.shape, F32), compiler_params=PARAMS
    )(a, b)


def z_kernel(parts_ref, factor_ref, out_ref):
    rows = []
    for t in range(4):
        lanes = slice(256 * t, 256 * t + 256)
        rows.append((parts_ref[0, :, lanes] + parts_ref[1, :, lanes]) + (parts_ref[2, :, lanes] + parts_ref[3, :, lanes]))
    top, low = split(jnp.concatenate(rows, axis=0))
    factor, rest = split(factor_ref[...])
    both = jnp.dot(jnp.concatenate([top, low], axis=0), factor, preferred_element_type=F32)
    both = both[0:192] + both[192:384] + jnp.dot(top, rest, preferred_element_type=F32)
    for t in range(4):
        for k in range(3):
            out_ref[pl.ds(4 * k + t, 48, stride=12), :] = both[48 * t : 48 * t + 48, 128 * k : 128 * k + 128]


def z_product(parts, factor):
    return pl.pallas_call(
        z_kernel, out_shape=jax.ShapeDtypeStruct((576, 128), F32), compiler_params=PARAMS
    )(parts, factor)


def copies_kernel(parts_ref, out_ref, both_ref):
    for h in range(2):
        both_ref[:, 4 * h : 4 * h + 4] = parts_ref[h].sum(0)
    for n in range(16):
        out_ref[n] = both_ref[...]


def copies(parts):
    return pl.pallas_call(
        copies_kernel,
        out_shape=jax.ShapeDtypeStruct((16, 9, 8, 128), F32),
        scratch_shapes=[pltpu.VMEM((9, 8, 128), F32)],
        compiler_params=PARAMS,
    )(parts)


def gram_kernel(both_ref, out_ref, terms_ref):
    x, y = lax.axis_index("x"), lax.axis_index("y")

    def rows_of(start, count, i):
        tiles = [both_ref[pl.ds(start, count), 3 * i + k].reshape(8 * count, 128) for k in range(3)]
        wide = jnp.concatenate(tiles, axis=1)
        return split(jnp.concatenate([wide[:, R * q : R * q + R] for q in range(4)], axis=0))

    total = jnp.zeros((256, 128), F32)
    for i in range(3):
        top, low = rows_of(8 * (x % 2), 8, i)
        right, rest = rows_of(4 * y, 4, i)
        total += dot_nt(top, right) + (dot_nt(low, right) + dot_nt(top, rest))
    terms_ref[...] = total
    first = (lax.broadcasted_iota(jnp.int32, (4, 128), 1) & 4) == 0
    for c in range(2):
        for k in range(4):
            for t in range(0, 4, 2):
                start = 32 * c + 8 * k + t + 4 * (x // 2)
                even = terms_ref[pl.ds(start, 4, stride=64), :]
                odd = terms_ref[pl.ds(start + 1, 4, stride=64), :]
                out_ref[c, 0, 2 * k + t // 2] = jnp.where(first, even, pltpu.roll(odd, 4, 1))
                out_ref[c, 1, 2 * k + t // 2] = jnp.where(first, pltpu.roll(even, 124, 1), odd)


def gram_terms(both):
    return pl.pallas_call(
        gram_kernel,
        out_shape=jax.ShapeDtypeStruct((2, 2, 8, 4, 128), F32),
        scratch_shapes=[pltpu.VMEM((256, 128), F32)],
        compiler_params=PARAMS,
    )(both)


def last_kernel(terms_ref, out_ref):
    total = terms_ref[...].sum(0)
    row = lax.broadcasted_iota(jnp.int32, (64, 128), 0)
    lane = lax.broadcasted_iota(jnp.int32, (64, 128), 1)
    source = (row & 3) * 32 + (row >> 4) * 8 + ((row >> 2) & 3)
    for half in range(2):
        pick = jnp.where(lane == source + 4 * half, 1.0, 0.0).astype(F32)
        moved = lax.dot_general(total, pick, (((1,), (1,)), ((), ())), precision=HIGHEST, preferred_element_type=F32)
        out_ref[4 * half : 4 * half + 4] = moved / (R * R)


def last(terms):
    return pl.pallas_call(
        last_kernel, out_shape=jax.ShapeDtypeStruct((8, 64), F32), compiler_params=PARAMS
    )(terms).T


def body(species, factor_y, factor_z):
    four_z = jnp.einsum("ab,zs->azbs", jnp.eye(4, dtype=F32), factor_z).reshape(256, 384)
    others, mine = y_product(species, factor_y)
    along_y = add(mine, lax.ppermute(others, "c", [(0, 1), (1, 0)]))
    parts = z_product(lax.all_to_all(along_y, "x", 0, 0, tiled=True), four_z)
    parts = lax.all_to_all(parts.reshape(144, 4, 128), ("h", "g"), 0, 0, tiled=True)
    both = copies(parts.reshape(2, 8, 9, 4, 128)).reshape(144, 8, 128)
    both = lax.all_to_all(both, ("y", "x"), 0, 0, tiled=True)
    terms = gram_terms(both.reshape(16, 9, 8, 128)).reshape(32, 4, 128)
    return last(lax.all_to_all(terms, ("c", "h", "g"), 0, 0, tiled=True))


def solution(mesh):
    fine = Mesh(mesh.devices.reshape(2, 4, 4, 2, 8), ("h", "y", "x", "c", "g"))
    placed = (P(("h", "y"), "g", ("x", "c")), P(("x", "c"), None), P("g", None))
    return jax.shard_map(
        body, mesh=fine, in_specs=placed, out_specs=P(("h", "y"), ("x", "c", "g")), check_vma=False
    )
```

```python
import jax
import jax.numpy as jnp
from jax import lax
from jax.experimental import pallas as pl
from jax.experimental.pallas import tpu as pltpu
from jax.sharding import Mesh, PartitionSpec as P

R = 96
HIGHEST = lax.Precision.HIGHEST
F32 = jnp.float32
BF16 = jnp.bfloat16
PARAMS = pltpu.CompilerParams(vmem_limit_bytes=32 * 1024 * 1024)


def split(value):
    top = value.astype(BF16)
    return top, (value - top.astype(F32)).astype(BF16)


def dot_nt(left, right):
    return lax.dot_general(left, right, (((1,), (1,)), ((), ())), preferred_element_type=F32)


def halves(rows):
    top, low = split(rows)
    upper = jnp.concatenate([top, top], axis=1)
    return jnp.concatenate([upper, jnp.concatenate([low, jnp.zeros_like(low)], axis=1)], axis=0)


def product(left, right):
    both = dot_nt(left, right)
    return both[0:48] + both[48:96]


def others_kernel(species_hbm, factor_hbm, others_ref, right_ref, left_ref, field_ref, factor_ref, sems):
    c = lax.axis_index("c")
    copies = [pltpu.make_async_copy(factor_hbm, factor_ref, sems.at[4])]
    for j in range(4):
        rows = pl.ds(16 * j, 16)
        copies.append(pltpu.make_async_copy(species_hbm.at[rows], field_ref.at[rows], sems.at[j]))
    for copy in copies:
        copy.start()
    copies[0].wait()
    left_ref[...] = halves(factor_ref[pl.ds(pl.multiple_of(48 * c, 48), 48)])
    left = halves(factor_ref[pl.ds(pl.multiple_of(48 * (1 - c), 48), 48)])
    for j in range(4):
        copies[1 + j].wait()
        top, low = split(field_ref[16 * j : 16 * j + 16].reshape(1024, 128))
        right = jnp.concatenate([top, low], axis=1)
        right_ref[j] = right
        others_ref[j] = product(left, right)


def others_product(species, factor_y):
    hbm = pl.BlockSpec(memory_space=pltpu.HBM)
    return pl.pallas_call(
        others_kernel,
        in_specs=[hbm, hbm],
        out_shape=[
            jax.ShapeDtypeStruct((4, 48, 1024), F32),
            pltpu.VMEM((4, 1024, 256), BF16),
            pltpu.VMEM((96, 256), BF16),
        ],
        scratch_shapes=[
            pltpu.VMEM((64, 64, 128), F32),
            pltpu.VMEM((R, 128), F32),
            pltpu.SemaphoreType.DMA((5,)),
        ],
        compiler_params=PARAMS,
    )(pltpu.with_memory_space_constraint(species, pltpu.HBM), pltpu.with_memory_space_constraint(factor_y.T, pltpu.HBM))


def early_kernel(left_ref, right_ref, factor_ref, out_ref, top_ref, low_ref, four_ref):
    four_ref[...] = jnp.zeros_like(four_ref)
    for q in range(4):
        four_ref[64 * q : 64 * q + 64, R * q : R * q + R] = factor_ref[...]
    top_ref[...], low_ref[...] = split(four_ref[...])

    @pl.when(lax.axis_index("c") == 1)
    def _():
        for j in range(4):
            out_ref[j] = product(left_ref[...], right_ref[j])


def early_product(left, right, factor_z):
    four = pltpu.VMEM((256, 384), BF16)
    return pl.pallas_call(
        early_kernel,
        out_shape=[pltpu.VMEM((4, 48, 1024), F32), four, four],
        scratch_shapes=[pltpu.VMEM((256, 384), F32)],
        compiler_params=PARAMS,
    )(left, right, factor_z)


def add_kernel(left_ref, right_ref, mine_ref, received_ref, out_ref):
    c = lax.axis_index("c")

    @pl.when(c == 0)
    def _():
        for j in range(4):
            out_ref[j] = product(left_ref[...], right_ref[j]) + received_ref[j]

    @pl.when(c == 1)
    def _():
        out_ref[...] = mine_ref[...] + received_ref[...]


def add(left, right, mine, received):
    return pl.pallas_call(
        add_kernel, out_shape=pltpu.VMEM(mine.shape, F32), compiler_params=PARAMS
    )(left, right, mine, received)


def z_kernel(parts_ref, factor_ref, rest_ref, out_ref):
    rows = []
    for t in range(4):
        lanes = slice(256 * t, 256 * t + 256)
        rows.append((parts_ref[0, :, lanes] + parts_ref[1, :, lanes]) + (parts_ref[2, :, lanes] + parts_ref[3, :, lanes]))
    top, low = split(jnp.concatenate(rows, axis=0))
    both = jnp.dot(jnp.concatenate([top, low], axis=0), factor_ref[...], preferred_element_type=F32)
    both = both[0:192] + both[192:384] + jnp.dot(top, rest_ref[...], preferred_element_type=F32)
    for t in range(4):
        for k in range(3):
            out_ref[pl.ds(4 * k + t, 48, stride=12), :] = both[48 * t : 48 * t + 48, 128 * k : 128 * k + 128]


def z_product(parts, factor, rest):
    return pl.pallas_call(
        z_kernel, out_shape=jax.ShapeDtypeStruct((576, 128), F32), compiler_params=PARAMS
    )(parts, factor, rest)


def copies_kernel(parts_ref, out_ref, both_ref):
    for h in range(2):
        both_ref[:, 4 * h : 4 * h + 4] = parts_ref[h].sum(0)
    for n in range(16):
        out_ref[n] = both_ref[...]


def copies(parts):
    return pl.pallas_call(
        copies_kernel,
        out_shape=jax.ShapeDtypeStruct((16, 9, 8, 128), F32),
        scratch_shapes=[pltpu.VMEM((9, 8, 128), F32)],
        compiler_params=PARAMS,
    )(parts)


def gram_kernel(both_ref, out_ref, terms_ref):
    x, y = lax.axis_index("x"), lax.axis_index("y")

    def rows_of(start, count, i):
        tiles = [both_ref[pl.ds(start, count), 3 * i + k].reshape(8 * count, 128) for k in range(3)]
        wide = jnp.concatenate(tiles, axis=1)
        return split(jnp.concatenate([wide[:, R * q : R * q + R] for q in range(4)], axis=0))

    total = jnp.zeros((256, 128), F32)
    for i in range(3):
        top, low = rows_of(8 * (x % 2), 8, i)
        right, rest = rows_of(4 * y, 4, i)
        total += dot_nt(top, right) + (dot_nt(low, right) + dot_nt(top, rest))
    terms_ref[...] = total
    first = (lax.broadcasted_iota(jnp.int32, (4, 128), 1) & 4) == 0
    for c in range(2):
        for k in range(4):
            for t in range(0, 4, 2):
                start = 32 * c + 8 * k + t + 4 * (x // 2)
                even = terms_ref[pl.ds(start, 4, stride=64), :]
                odd = terms_ref[pl.ds(start + 1, 4, stride=64), :]
                out_ref[c, 0, 2 * k + t // 2] = jnp.where(first, even, pltpu.roll(odd, 4, 1))
                out_ref[c, 1, 2 * k + t // 2] = jnp.where(first, pltpu.roll(even, 124, 1), odd)


def gram_terms(both):
    return pl.pallas_call(
        gram_kernel,
        out_shape=jax.ShapeDtypeStruct((2, 2, 8, 4, 128), F32),
        scratch_shapes=[pltpu.VMEM((256, 128), F32)],
        compiler_params=PARAMS,
    )(both)


def last_kernel(terms_ref, out_ref):
    total = terms_ref[...].sum(0)
    row = lax.broadcasted_iota(jnp.int32, (64, 128), 0)
    lane = lax.broadcasted_iota(jnp.int32, (64, 128), 1)
    source = (row & 3) * 32 + (row >> 4) * 8 + ((row >> 2) & 3)
    for half in range(2):
        pick = jnp.where(lane == source + 4 * half, 1.0, 0.0).astype(F32)
        moved = lax.dot_general(total, pick, (((1,), (1,)), ((), ())), precision=HIGHEST, preferred_element_type=F32)
        out_ref[4 * half : 4 * half + 4] = moved / (R * R)


def last(terms):
    return pl.pallas_call(
        last_kernel, out_shape=jax.ShapeDtypeStruct((8, 64), F32), compiler_params=PARAMS
    )(terms).T


def body(species, factor_y, factor_z):
    others, right, left = others_product(species, factor_y)
    mine, factor, rest = early_product(left, right, factor_z)
    along_y = add(left, right, mine, lax.ppermute(others, "c", [(0, 1), (1, 0)]))
    parts = z_product(lax.all_to_all(along_y, "x", 0, 0, tiled=True), factor, rest)
    parts = lax.all_to_all(parts.reshape(144, 4, 128), ("h", "g"), 0, 0, tiled=True)
    both = copies(parts.reshape(2, 8, 9, 4, 128)).reshape(144, 8, 128)
    both = lax.all_to_all(both, ("y", "x"), 0, 0, tiled=True)
    terms = gram_terms(both.reshape(16, 9, 8, 128)).reshape(32, 4, 128)
    return last(lax.all_to_all(terms, ("c", "h", "g"), 0, 0, tiled=True))


def solution(mesh):
    fine = Mesh(mesh.devices.reshape(2, 4, 4, 2, 8), ("h", "y", "x", "c", "g"))
    placed = (P(("h", "y"), "g", ("x", "c")), P(("x", "c"), None), P("g", None))
    return jax.shard_map(
        body, mesh=fine, in_specs=placed, out_specs=P(("h", "y"), ("x", "c", "g")), check_vma=False
    )
```

```python
import jax
import jax.numpy as jnp
from jax import lax
from jax.experimental import pallas as pl
from jax.experimental.pallas import tpu as pltpu
from jax.sharding import Mesh, PartitionSpec as P

R = 96
HIGHEST = lax.Precision.HIGHEST
F32 = jnp.float32
BF16 = jnp.bfloat16
PARAMS = pltpu.CompilerParams(vmem_limit_bytes=32 * 1024 * 1024)


def split(value):
    top = value.astype(BF16)
    return top, (value - top.astype(F32)).astype(BF16)


def dot_nt(left, right):
    return lax.dot_general(left, right, (((1,), (1,)), ((), ())), preferred_element_type=F32)


def product(rows, field):
    top, low = split(rows)
    upper = jnp.concatenate([top, top], axis=1)
    left = jnp.concatenate([upper, jnp.concatenate([low, jnp.zeros_like(low)], axis=1)], axis=0)
    top, low = split(field.reshape(1024, 128))
    both = dot_nt(left, jnp.concatenate([top, low], axis=1))
    return both[0:48] + both[48:96]


def rows_for(core, factor_ref):
    return factor_ref[pl.ds(pl.multiple_of(48 * core, 48), 48)]


def others_kernel(species_hbm, factor_hbm, others_ref, field_ref, factor_ref, sems):
    copies = [pltpu.make_async_copy(factor_hbm, factor_ref, sems.at[4])]
    for j in range(4):
        rows = pl.ds(16 * j, 16)
        copies.append(pltpu.make_async_copy(species_hbm.at[rows], field_ref.at[rows], sems.at[j]))
    for copy in copies:
        copy.start()
    copies[0].wait()
    rows = rows_for(1 - lax.axis_index("c"), factor_ref)
    for j in range(4):
        copies[1 + j].wait()
        others_ref[j] = product(rows, field_ref[16 * j : 16 * j + 16])


def others_product(species, factor_y):
    hbm = pl.BlockSpec(memory_space=pltpu.HBM)
    return pl.pallas_call(
        others_kernel,
        in_specs=[hbm, hbm],
        out_shape=[
            jax.ShapeDtypeStruct((4, 48, 1024), F32),
            pltpu.VMEM((64, 64, 128), F32),
            pltpu.VMEM((R, 128), F32),
        ],
        scratch_shapes=[pltpu.SemaphoreType.DMA((5,))],
        compiler_params=PARAMS,
    )(pltpu.with_memory_space_constraint(species, pltpu.HBM), pltpu.with_memory_space_constraint(factor_y.T, pltpu.HBM))


def early_kernel(field_ref, factor_y_ref, factor_ref, out_ref, top_ref, low_ref, four_ref):
    four_ref[...] = jnp.zeros_like(four_ref)
    for q in range(4):
        four_ref[64 * q : 64 * q + 64, R * q : R * q + R] = factor_ref[...]
    top_ref[...], low_ref[...] = split(four_ref[...])

    @pl.when(lax.axis_index("c") == 1)
    def _():
        for j in range(4):
            out_ref[j] = product(rows_for(1, factor_y_ref), field_ref[16 * j : 16 * j + 16])


def early_product(field, factor_y, factor_z):
    four = pltpu.VMEM((256, 384), BF16)
    return pl.pallas_call(
        early_kernel,
        out_shape=[pltpu.VMEM((4, 48, 1024), F32), four, four],
        scratch_shapes=[pltpu.VMEM((256, 384), F32)],
        compiler_params=PARAMS,
    )(field, factor_y, factor_z)


def add_kernel(field_ref, factor_ref, mine_ref, received_ref, out_ref):
    c = lax.axis_index("c")

    @pl.when(c == 0)
    def _():
        for j in range(4):
            field = field_ref[16 * j : 16 * j + 16].reshape(1024, 128)
            own = lax.dot_general(
                rows_for(0, factor_ref), field, (((1,), (1,)), ((), ())), precision=HIGHEST, preferred_element_type=F32
            )
            out_ref[j] = own + received_ref[j]

    @pl.when(c == 1)
    def _():
        out_ref[...] = mine_ref[...] + received_ref[...]


def add(field, factor, mine, received):
    return pl.pallas_call(
        add_kernel, out_shape=pltpu.VMEM(mine.shape, F32), compiler_params=PARAMS
    )(field, factor, mine, received)


def z_kernel(parts_ref, factor_ref, rest_ref, out_ref):
    rows = []
    for t in range(4):
        lanes = slice(256 * t, 256 * t + 256)
        rows.append((parts_ref[0, :, lanes] + parts_ref[1, :, lanes]) + (parts_ref[2, :, lanes] + parts_ref[3, :, lanes]))
    top, low = split(jnp.concatenate(rows, axis=0))
    both = jnp.dot(jnp.concatenate([top, low], axis=0), factor_ref[...], preferred_element_type=F32)
    both = both[0:192] + both[192:384] + jnp.dot(top, rest_ref[...], preferred_element_type=F32)
    for t in range(4):
        for k in range(3):
            out_ref[pl.ds(4 * k + t, 48, stride=12), :] = both[48 * t : 48 * t + 48, 128 * k : 128 * k + 128]


def z_product(parts, factor, rest):
    return pl.pallas_call(
        z_kernel, out_shape=jax.ShapeDtypeStruct((576, 128), F32), compiler_params=PARAMS
    )(parts, factor, rest)


def copies_kernel(parts_ref, out_ref, both_ref):
    for h in range(2):
        both_ref[:, 4 * h : 4 * h + 4] = parts_ref[h].sum(0)
    for n in range(16):
        out_ref[n] = both_ref[...]


def copies(parts):
    return pl.pallas_call(
        copies_kernel,
        out_shape=jax.ShapeDtypeStruct((16, 9, 8, 128), F32),
        scratch_shapes=[pltpu.VMEM((9, 8, 128), F32)],
        compiler_params=PARAMS,
    )(parts)


def gram_kernel(both_ref, out_ref, terms_ref):
    x, y = lax.axis_index("x"), lax.axis_index("y")

    def rows_of(start, count, i):
        tiles = [both_ref[pl.ds(start, count), 3 * i + k].reshape(8 * count, 128) for k in range(3)]
        wide = jnp.concatenate(tiles, axis=1)
        return split(jnp.concatenate([wide[:, R * q : R * q + R] for q in range(4)], axis=0))

    total = jnp.zeros((256, 128), F32)
    for i in range(3):
        top, low = rows_of(8 * (x % 2), 8, i)
        right, rest = rows_of(4 * y, 4, i)
        total += dot_nt(top, right) + (dot_nt(low, right) + dot_nt(top, rest))
    terms_ref[...] = total
    first = (lax.broadcasted_iota(jnp.int32, (4, 128), 1) & 4) == 0
    for c in range(2):
        for k in range(4):
            for t in range(0, 4, 2):
                start = 32 * c + 8 * k + t + 4 * (x // 2)
                even = terms_ref[pl.ds(start, 4, stride=64), :]
                odd = terms_ref[pl.ds(start + 1, 4, stride=64), :]
                out_ref[c, 0, 2 * k + t // 2] = jnp.where(first, even, pltpu.roll(odd, 4, 1))
                out_ref[c, 1, 2 * k + t // 2] = jnp.where(first, pltpu.roll(even, 124, 1), odd)


def gram_terms(both):
    return pl.pallas_call(
        gram_kernel,
        out_shape=jax.ShapeDtypeStruct((2, 2, 8, 4, 128), F32),
        scratch_shapes=[pltpu.VMEM((256, 128), F32)],
        compiler_params=PARAMS,
    )(both)


def last_kernel(terms_ref, out_ref):
    total = terms_ref[...].sum(0)
    row = lax.broadcasted_iota(jnp.int32, (64, 128), 0)
    lane = lax.broadcasted_iota(jnp.int32, (64, 128), 1)
    source = (row & 3) * 32 + (row >> 4) * 8 + ((row >> 2) & 3)
    for half in range(2):
        pick = jnp.where(lane == source + 4 * half, 1.0, 0.0).astype(F32)
        moved = lax.dot_general(total, pick, (((1,), (1,)), ((), ())), precision=HIGHEST, preferred_element_type=F32)
        out_ref[4 * half : 4 * half + 4] = moved / (R * R)


def last(terms):
    return pl.pallas_call(
        last_kernel, out_shape=jax.ShapeDtypeStruct((8, 64), F32), compiler_params=PARAMS
    )(terms).T


def body(species, factor_y, factor_z):
    others, field, factor_y = others_product(species, factor_y)
    mine, factor, rest = early_product(field, factor_y, factor_z)
    along_y = add(field, factor_y, mine, lax.ppermute(others, "c", [(0, 1), (1, 0)]))
    parts = z_product(lax.all_to_all(along_y, "x", 0, 0, tiled=True), factor, rest)
    parts = lax.all_to_all(parts.reshape(144, 4, 128), ("h", "g"), 0, 0, tiled=True)
    both = copies(parts.reshape(2, 8, 9, 4, 128)).reshape(144, 8, 128)
    both = lax.all_to_all(both, ("y", "x"), 0, 0, tiled=True)
    terms = gram_terms(both.reshape(16, 9, 8, 128)).reshape(32, 4, 128)
    return last(lax.all_to_all(terms, ("c", "h", "g"), 0, 0, tiled=True))


def solution(mesh):
    fine = Mesh(mesh.devices.reshape(2, 4, 4, 2, 8), ("h", "y", "x", "c", "g"))
    placed = (P(("h", "y"), "g", ("x", "c")), P(("x", "c"), None), P("g", None))
    return jax.shard_map(
        body, mesh=fine, in_specs=placed, out_specs=P(("h", "y"), ("x", "c", "g")), check_vma=False
    )
```

```python
import jax
import jax.numpy as jnp
from jax import lax
from jax.experimental import pallas as pl
from jax.experimental.pallas import tpu as pltpu
from jax.sharding import Mesh, PartitionSpec as P

R = 96
HIGHEST = lax.Precision.HIGHEST
F32 = jnp.float32
BF16 = jnp.bfloat16
PARAMS = pltpu.CompilerParams(vmem_limit_bytes=32 * 1024 * 1024)


def split(value):
    top = value.astype(BF16)
    return top, (value - top.astype(F32)).astype(BF16)


def dot_nt(left, right):
    return lax.dot_general(left, right, (((1,), (1,)), ((), ())), preferred_element_type=F32)


def halves(rows):
    top, low = split(rows)
    upper = jnp.concatenate([top, top], axis=1)
    return jnp.concatenate([upper, jnp.concatenate([low, jnp.zeros_like(low)], axis=1)], axis=0)


def product(left, field):
    top, low = split(field.reshape(-1, 128))
    both = dot_nt(left, jnp.concatenate([top, low], axis=1))
    return both[0:48] + both[48:96]


def rows_for(core, factor_ref):
    return factor_ref[pl.ds(pl.multiple_of(48 * core, 48), 48)]


def others_kernel(species_hbm, factor_hbm, others_ref, field_ref, factor_ref, sems):
    copies = [pltpu.make_async_copy(factor_hbm, factor_ref, sems.at[2])]
    for j in range(2):
        rows = pl.ds(32 * j, 32)
        copies.append(pltpu.make_async_copy(species_hbm.at[rows], field_ref.at[rows], sems.at[j]))
    for copy in copies:
        copy.start()
    copies[0].wait()
    left = halves(rows_for(1 - lax.axis_index("c"), factor_ref))
    for j in range(4):
        if j % 2 == 0:
            copies[1 + j // 2].wait()
        others_ref[j] = product(left, field_ref[16 * j : 16 * j + 16])


def others_product(species, factor_y):
    hbm = pl.BlockSpec(memory_space=pltpu.HBM)
    return pl.pallas_call(
        others_kernel,
        in_specs=[hbm, hbm],
        out_shape=[
            jax.ShapeDtypeStruct((4, 48, 1024), F32),
            pltpu.VMEM((64, 64, 128), F32),
            pltpu.VMEM((R, 128), F32),
        ],
        scratch_shapes=[pltpu.SemaphoreType.DMA((3,))],
        compiler_params=PARAMS,
    )(pltpu.with_memory_space_constraint(species, pltpu.HBM), pltpu.with_memory_space_constraint(factor_y.T, pltpu.HBM))


def early_kernel(field_ref, factor_y_ref, factor_ref, out_ref, top_ref, low_ref, four_ref):
    four_ref[...] = jnp.zeros_like(four_ref)
    for q in range(4):
        four_ref[64 * q : 64 * q + 64, R * q : R * q + R] = factor_ref[...]
    top_ref[...], low_ref[...] = split(four_ref[...])

    @pl.when(lax.axis_index("c") == 1)
    def _():
        left = halves(rows_for(1, factor_y_ref))
        for j in range(4):
            out_ref[j] = product(left, field_ref[16 * j : 16 * j + 16])


def early_product(field, factor_y, factor_z):
    four = pltpu.VMEM((256, 384), BF16)
    return pl.pallas_call(
        early_kernel,
        out_shape=[pltpu.VMEM((4, 48, 1024), F32), four, four],
        scratch_shapes=[pltpu.VMEM((256, 384), F32)],
        compiler_params=PARAMS,
    )(field, factor_y, factor_z)


def add_kernel(field_ref, factor_ref, mine_ref, received_ref, out_ref):
    c = lax.axis_index("c")

    @pl.when(c == 0)
    def _():
        for j in range(4):
            field = field_ref[16 * j : 16 * j + 16].reshape(1024, 128)
            own = lax.dot_general(
                rows_for(0, factor_ref), field, (((1,), (1,)), ((), ())), precision=HIGHEST, preferred_element_type=F32
            )
            out_ref[j] = own + received_ref[j]

    @pl.when(c == 1)
    def _():
        out_ref[...] = mine_ref[...] + received_ref[...]


def add(field, factor, mine, received):
    return pl.pallas_call(
        add_kernel, out_shape=pltpu.VMEM(mine.shape, F32), compiler_params=PARAMS
    )(field, factor, mine, received)


def z_kernel(parts_ref, factor_ref, rest_ref, out_ref):
    rows = []
    for t in range(4):
        lanes = slice(256 * t, 256 * t + 256)
        rows.append((parts_ref[0, :, lanes] + parts_ref[1, :, lanes]) + (parts_ref[2, :, lanes] + parts_ref[3, :, lanes]))
    top, low = split(jnp.concatenate(rows, axis=0))
    both = jnp.dot(jnp.concatenate([top, low], axis=0), factor_ref[...], preferred_element_type=F32)
    both = both[0:192] + both[192:384] + jnp.dot(top, rest_ref[...], preferred_element_type=F32)
    for t in range(4):
        for k in range(3):
            out_ref[pl.ds(4 * k + t, 48, stride=12), :] = both[48 * t : 48 * t + 48, 128 * k : 128 * k + 128]


def z_product(parts, factor, rest):
    return pl.pallas_call(
        z_kernel, out_shape=jax.ShapeDtypeStruct((576, 128), F32), compiler_params=PARAMS
    )(parts, factor, rest)


def copies_kernel(parts_ref, out_ref, both_ref):
    for h in range(2):
        both_ref[:, 4 * h : 4 * h + 4] = parts_ref[h].sum(0)
    for n in range(16):
        out_ref[n] = both_ref[...]


def copies(parts):
    return pl.pallas_call(
        copies_kernel,
        out_shape=jax.ShapeDtypeStruct((16, 9, 8, 128), F32),
        scratch_shapes=[pltpu.VMEM((9, 8, 128), F32)],
        compiler_params=PARAMS,
    )(parts)


def gram_kernel(both_ref, out_ref, terms_ref):
    x, y = lax.axis_index("x"), lax.axis_index("y")

    def rows_of(start, count, i):
        tiles = [both_ref[pl.ds(start, count), 3 * i + k].reshape(8 * count, 128) for k in range(3)]
        wide = jnp.concatenate(tiles, axis=1)
        return split(jnp.concatenate([wide[:, R * q : R * q + R] for q in range(4)], axis=0))

    total = jnp.zeros((256, 128), F32)
    for i in range(3):
        top, low = rows_of(8 * (x % 2), 8, i)
        right, rest = rows_of(4 * y, 4, i)
        total += dot_nt(top, right) + (dot_nt(low, right) + dot_nt(top, rest))
    terms_ref[0:256] = total
    first = (lax.broadcasted_iota(jnp.int32, (4, 128), 1) & 4) == 0
    for c in range(2):
        for k in range(4):
            for t in range(0, 4, 2):
                start = 32 * c + 8 * k + t + 4 * (x // 2)
                even = terms_ref[pl.ds(start, 4, stride=64), :]
                odd = terms_ref[pl.ds(start + 1, 4, stride=64), :]
                out_ref[c, 0, 2 * k + t // 2] = jnp.where(first, even, pltpu.roll(odd, 4, 1))
                out_ref[c, 1, 2 * k + t // 2] = jnp.where(first, pltpu.roll(even, 124, 1), odd)


def gram_terms(both):
    return pl.pallas_call(
        gram_kernel,
        out_shape=jax.ShapeDtypeStruct((2, 2, 8, 4, 128), F32),
        scratch_shapes=[pltpu.VMEM((320, 128), F32)],
        compiler_params=PARAMS,
    )(both)


def last_kernel(terms_ref, out_ref):
    total = terms_ref[...].sum(0)
    row = lax.broadcasted_iota(jnp.int32, (64, 128), 0)
    lane = lax.broadcasted_iota(jnp.int32, (64, 128), 1)
    source = (row & 3) * 32 + (row >> 4) * 8 + ((row >> 2) & 3)
    for half in range(2):
        pick = jnp.where(lane == source + 4 * half, 1.0, 0.0).astype(F32)
        moved = lax.dot_general(total, pick, (((1,), (1,)), ((), ())), precision=HIGHEST, preferred_element_type=F32)
        out_ref[4 * half : 4 * half + 4] = moved / (R * R)


def last(terms):
    return pl.pallas_call(
        last_kernel, out_shape=jax.ShapeDtypeStruct((8, 64), F32), compiler_params=PARAMS
    )(terms).T


def body(species, factor_y, factor_z):
    others, field, factor_y = others_product(species, factor_y)
    mine, factor, rest = early_product(field, factor_y, factor_z)
    along_y = add(field, factor_y, mine, lax.ppermute(others, "c", [(0, 1), (1, 0)]))
    parts = z_product(lax.all_to_all(along_y, "x", 0, 0, tiled=True), factor, rest)
    parts = lax.all_to_all(parts.reshape(144, 4, 128), ("h", "g"), 0, 0, tiled=True)
    both = copies(parts.reshape(2, 8, 9, 4, 128)).reshape(144, 8, 128)
    both = lax.all_to_all(both, ("y", "x"), 0, 0, tiled=True)
    terms = gram_terms(both.reshape(16, 9, 8, 128)).reshape(32, 4, 128)
    return last(lax.all_to_all(terms, ("c", "h", "g"), 0, 0, tiled=True))


def solution(mesh):
    fine = Mesh(mesh.devices.reshape(2, 4, 4, 2, 8), ("h", "y", "x", "c", "g"))
    placed = (P(("h", "y"), "g", ("x", "c")), P(("x", "c"), None), P("g", None))
    return jax.shard_map(
        body, mesh=fine, in_specs=placed, out_specs=P(("h", "y"), ("x", "c", "g")), check_vma=False
    )
```

```python
import jax
import jax.numpy as jnp
from jax import lax
from jax.experimental import pallas as pl
from jax.experimental.pallas import tpu as pltpu
from jax.sharding import Mesh, PartitionSpec as P

R = 96
HIGHEST = lax.Precision.HIGHEST
F32 = jnp.float32
BF16 = jnp.bfloat16
PARAMS = pltpu.CompilerParams(vmem_limit_bytes=32 * 1024 * 1024)


def split(value):
    top = value.astype(BF16)
    return top, (value - top.astype(F32)).astype(BF16)


def dot_nt(left, right):
    return lax.dot_general(left, right, (((1,), (1,)), ((), ())), preferred_element_type=F32)


def halves(rows):
    top, low = split(rows)
    upper = jnp.concatenate([top, top], axis=1)
    return jnp.concatenate([upper, jnp.concatenate([low, jnp.zeros_like(low)], axis=1)], axis=0)


def product(left, field):
    top, low = split(field.reshape(-1, 128))
    both = dot_nt(left, jnp.concatenate([top, low], axis=1))
    return both[0:48] + both[48:96]


def rows_for(core, factor_ref):
    return factor_ref[pl.ds(pl.multiple_of(48 * core, 48), 48)]


def others_kernel(species_hbm, factor_hbm, others_ref, field_ref, factor_ref, sems):
    copies = [pltpu.make_async_copy(factor_hbm, factor_ref, sems.at[2])]
    for j in range(2):
        rows = pl.ds(32 * j, 32)
        copies.append(pltpu.make_async_copy(species_hbm.at[rows], field_ref.at[rows], sems.at[j]))
    for copy in copies:
        copy.start()
    copies[0].wait()
    left = halves(rows_for(1 - lax.axis_index("c"), factor_ref))
    for j in range(4):
        if j % 2 == 0:
            copies[1 + j // 2].wait()
        others_ref[j] = product(left, field_ref[16 * j : 16 * j + 16])


def others_product(species, factor_y):
    hbm = pl.BlockSpec(memory_space=pltpu.HBM)
    return pl.pallas_call(
        others_kernel,
        in_specs=[hbm, hbm],
        out_shape=[
            jax.ShapeDtypeStruct((4, 48, 1024), F32),
            pltpu.VMEM((64, 64, 128), F32),
            pltpu.VMEM((R, 128), F32),
        ],
        scratch_shapes=[pltpu.SemaphoreType.DMA((3,))],
        compiler_params=PARAMS,
    )(pltpu.with_memory_space_constraint(species, pltpu.HBM), pltpu.with_memory_space_constraint(factor_y.T, pltpu.HBM))


def set_up(factor_ref, top_ref, low_ref, pick_ref, four_ref):
    four_ref[...] = jnp.zeros_like(four_ref)
    for q in range(4):
        four_ref[64 * q : 64 * q + 64, R * q : R * q + R] = factor_ref[...]
    top_ref[...], low_ref[...] = split(four_ref[...])
    row = lax.broadcasted_iota(jnp.int32, (128, 128), 0)
    lane = lax.broadcasted_iota(jnp.int32, (128, 128), 1)
    source = (row & 3) * 32 + ((row >> 4) & 3) * 8 + (row >> 6) * 4 + ((row >> 2) & 3)
    pick_ref[...] = jnp.where(lane == source, 1.0, 0.0).astype(F32)


FOUR = pltpu.VMEM((256, 384), BF16)
PICK = pltpu.VMEM((128, 128), F32)
HALF = pltpu.VMEM((4, 48, 1024), F32)


def early_kernel(field_ref, factor_y_ref, factor_ref, out_ref, top_ref, low_ref, pick_ref, four_ref):
    @pl.when(lax.axis_index("c") == 1)
    def _():
        set_up(factor_ref, top_ref, low_ref, pick_ref, four_ref)
        left = halves(rows_for(1, factor_y_ref))
        for j in range(4):
            out_ref[j] = product(left, field_ref[16 * j : 16 * j + 16])


def early_product(field, factor_y, factor_z):
    return pl.pallas_call(
        early_kernel,
        out_shape=[HALF, FOUR, FOUR, PICK],
        scratch_shapes=[pltpu.VMEM((256, 384), F32)],
        compiler_params=PARAMS,
    )(field, factor_y, factor_z)


def add_kernel(
    field_ref, factor_y_ref, factor_ref, received_ref, mine_ref, top_in, low_in, pick_in, out_ref, top_ref, low_ref, pick_ref, four_ref
):
    c = lax.axis_index("c")

    @pl.when(c == 0)
    def _():
        set_up(factor_ref, top_ref, low_ref, pick_ref, four_ref)
        for j in range(4):
            field = field_ref[16 * j : 16 * j + 16].reshape(1024, 128)
            own = lax.dot_general(
                rows_for(0, factor_y_ref), field, (((1,), (1,)), ((), ())), precision=HIGHEST, preferred_element_type=F32
            )
            out_ref[j] = own + received_ref[j]

    @pl.when(c == 1)
    def _():
        out_ref[...] = mine_ref[...] + received_ref[...]


def add(field, factor_y, factor_z, received, early):
    return pl.pallas_call(
        add_kernel,
        out_shape=[HALF, FOUR, FOUR, PICK],
        scratch_shapes=[pltpu.VMEM((256, 384), F32)],
        input_output_aliases={5: 1, 6: 2, 7: 3},
        compiler_params=PARAMS,
    )(field, factor_y, factor_z, received, *early)


def z_kernel(parts_ref, factor_ref, rest_ref, out_ref):
    rows = []
    for t in range(4):
        lanes = slice(256 * t, 256 * t + 256)
        rows.append((parts_ref[0, :, lanes] + parts_ref[1, :, lanes]) + (parts_ref[2, :, lanes] + parts_ref[3, :, lanes]))
    top, low = split(jnp.concatenate(rows, axis=0))
    both = jnp.dot(jnp.concatenate([top, low], axis=0), factor_ref[...], preferred_element_type=F32)
    both = both[0:192] + both[192:384] + jnp.dot(top, rest_ref[...], preferred_element_type=F32)
    for t in range(4):
        for k in range(3):
            out_ref[pl.ds(4 * k + t, 48, stride=12), :] = both[48 * t : 48 * t + 48, 128 * k : 128 * k + 128]


def z_product(parts, factor, rest):
    return pl.pallas_call(
        z_kernel, out_shape=jax.ShapeDtypeStruct((576, 128), F32), compiler_params=PARAMS
    )(parts, factor, rest)


def copies_kernel(parts_ref, out_ref, both_ref):
    for h in range(2):
        both_ref[:, 4 * h : 4 * h + 4] = parts_ref[:, h].sum(0)
    for n in range(16):
        out_ref[n] = both_ref[...]


def copies(parts):
    return pl.pallas_call(
        copies_kernel,
        out_shape=jax.ShapeDtypeStruct((16, 9, 8, 128), F32),
        scratch_shapes=[pltpu.VMEM((9, 8, 128), F32)],
        compiler_params=PARAMS,
    )(parts)


def gram_kernel(both_ref, out_ref, terms_ref):
    x, y = lax.axis_index("x"), lax.axis_index("y")

    def rows_of(start, count, i):
        tiles = [both_ref[pl.ds(start, count), 3 * i + k].reshape(8 * count, 128) for k in range(3)]
        wide = jnp.concatenate(tiles, axis=1)
        return split(jnp.concatenate([wide[:, R * q : R * q + R] for q in range(4)], axis=0))

    total = jnp.zeros((256, 128), F32)
    for i in range(3):
        top, low = rows_of(8 * (x % 2), 8, i)
        right, rest = rows_of(4 * y, 4, i)
        total += dot_nt(top, right) + (dot_nt(low, right) + dot_nt(top, rest))
    terms_ref[0:256] = total
    first = (lax.broadcasted_iota(jnp.int32, (4, 128), 1) & 4) == 0
    for c in range(2):
        for k in range(4):
            for t in range(0, 4, 2):
                start = 32 * c + 8 * k + t + 4 * (x // 2)
                even = terms_ref[pl.ds(start, 4, stride=64), :]
                odd = terms_ref[pl.ds(start + 1, 4, stride=64), :]
                out_ref[2 * k + t // 2, 0, c] = jnp.where(first, even, pltpu.roll(odd, 4, 1))
                out_ref[2 * k + t // 2, 1, c] = jnp.where(first, pltpu.roll(even, 124, 1), odd)


def gram_terms(both):
    return pl.pallas_call(
        gram_kernel,
        out_shape=jax.ShapeDtypeStruct((8, 2, 2, 4, 128), F32),
        scratch_shapes=[pltpu.VMEM((320, 128), F32)],
        compiler_params=PARAMS,
    )(both)


def last_kernel(terms_ref, pick_ref, out_ref):
    total = terms_ref[...].sum(0)
    moved = lax.dot_general(
        total, pick_ref[...], (((1,), (1,)), ((), ())), precision=HIGHEST, preferred_element_type=F32
    ) / (R * R)
    out_ref[0:4] = moved[:, 0:64]
    out_ref[4:8] = moved[:, 64:128]


def last(terms, pick):
    return pl.pallas_call(
        last_kernel, out_shape=jax.ShapeDtypeStruct((8, 64), F32), compiler_params=PARAMS
    )(terms, pick).T


def body(species, factor_y, factor_z):
    others, field, factor_y = others_product(species, factor_y)
    early = early_product(field, factor_y, factor_z)
    along_y, factor, rest, pick = add(
        field, factor_y, factor_z, lax.ppermute(others, "c", [(0, 1), (1, 0)]), early
    )
    parts = z_product(lax.all_to_all(along_y, "x", 0, 0, tiled=True), factor, rest)
    parts = lax.all_to_all(parts.reshape(144, 4, 128), ("g", "h"), 0, 0, tiled=True)
    both = copies(parts.reshape(8, 2, 9, 4, 128)).reshape(144, 8, 128)
    both = lax.all_to_all(both, ("y", "x"), 0, 0, tiled=True)
    terms = gram_terms(both.reshape(16, 9, 8, 128)).reshape(32, 4, 128)
    return last(lax.all_to_all(terms, ("g", "h", "c"), 0, 0, tiled=True), pick)


def solution(mesh):
    fine = Mesh(mesh.devices.reshape(2, 4, 4, 2, 8), ("h", "y", "x", "c", "g"))
    placed = (P(("h", "y"), "g", ("x", "c")), P(("x", "c"), None), P("g", None))
    return jax.shard_map(
        body, mesh=fine, in_specs=placed, out_specs=P(("h", "y"), ("x", "c", "g")), check_vma=False
    )
```

```python
import jax
import jax.numpy as jnp
from jax import lax
from jax.experimental import pallas as pl
from jax.experimental.pallas import tpu as pltpu
from jax.sharding import Mesh, PartitionSpec as P

R = 96
HIGHEST = lax.Precision.HIGHEST
F32 = jnp.float32
BF16 = jnp.bfloat16
PARAMS = pltpu.CompilerParams(vmem_limit_bytes=32 * 1024 * 1024)


def split(value):
    top = value.astype(BF16)
    return top, (value - top.astype(F32)).astype(BF16)


def dot_nt(left, right):
    return lax.dot_general(left, right, (((1,), (1,)), ((), ())), preferred_element_type=F32)


def halves(rows):
    top, low = split(rows)
    upper = jnp.concatenate([top, top], axis=1)
    return jnp.concatenate([upper, jnp.concatenate([low, jnp.zeros_like(low)], axis=1)], axis=0)


def product(left, field):
    top, low = split(field.reshape(-1, 128))
    both = dot_nt(left, jnp.concatenate([top, low], axis=1))
    return both[0:48] + both[48:96]


def rows_for(core, factor_ref):
    return factor_ref[pl.ds(pl.multiple_of(48 * core, 48), 48)]


def others_kernel(species_hbm, factor_hbm, others_ref, field_ref, factor_ref, sems):
    copies = [pltpu.make_async_copy(factor_hbm, factor_ref, sems.at[2])]
    for j in range(2):
        rows = pl.ds(32 * j, 32)
        copies.append(pltpu.make_async_copy(species_hbm.at[rows], field_ref.at[rows], sems.at[j]))
    for copy in copies:
        copy.start()
    copies[0].wait()
    left = halves(rows_for(1 - lax.axis_index("c"), factor_ref))
    for j in range(4):
        if j % 2 == 0:
            copies[1 + j // 2].wait()
        others_ref[j] = product(left, field_ref[16 * j : 16 * j + 16])


def others_product(species, factor_y):
    hbm = pl.BlockSpec(memory_space=pltpu.HBM)
    return pl.pallas_call(
        others_kernel,
        in_specs=[hbm, hbm],
        out_shape=[
            jax.ShapeDtypeStruct((4, 48, 1024), F32),
            pltpu.VMEM((64, 64, 128), F32),
            pltpu.VMEM((R, 128), F32),
        ],
        scratch_shapes=[pltpu.SemaphoreType.DMA((3,))],
        compiler_params=PARAMS,
    )(pltpu.with_memory_space_constraint(species, pltpu.HBM), pltpu.with_memory_space_constraint(factor_y.T, pltpu.HBM))


def set_up(factor_ref, top_ref, low_ref, pick_ref, four_ref):
    four_ref[...] = jnp.zeros_like(four_ref)
    for q in range(4):
        four_ref[64 * q : 64 * q + 64, R * q : R * q + R] = factor_ref[...]
    top_ref[...], low_ref[...] = split(four_ref[...])
    row = lax.broadcasted_iota(jnp.int32, (128, 128), 0)
    lane = lax.broadcasted_iota(jnp.int32, (128, 128), 1)
    source = (row & 3) * 32 + ((row >> 4) & 3) * 8 + (row >> 6) * 4 + ((row >> 2) & 3)
    pick_ref[...] = jnp.where(lane == source, 1.0, 0.0).astype(F32)


FOUR = pltpu.VMEM((256, 384), BF16)
PICK = pltpu.VMEM((128, 128), F32)
HALF = pltpu.VMEM((4, 48, 1024), F32)


def early_kernel(field_ref, factor_y_ref, factor_ref, out_ref, top_ref, low_ref, pick_ref, four_ref):
    @pl.when(lax.axis_index("c") == 1)
    def _():
        set_up(factor_ref, top_ref, low_ref, pick_ref, four_ref)
        left = halves(rows_for(1, factor_y_ref))
        for j in range(4):
            out_ref[j] = product(left, field_ref[16 * j : 16 * j + 16])


def early_product(field, factor_y, factor_z):
    return pl.pallas_call(
        early_kernel,
        out_shape=[HALF, FOUR, FOUR, PICK],
        scratch_shapes=[pltpu.VMEM((256, 384), F32)],
        compiler_params=PARAMS,
    )(field, factor_y, factor_z)


def add_kernel(
    field_ref, factor_y_ref, factor_ref, received_ref, mine_ref, top_in, low_in, pick_in, out_ref, top_ref, low_ref, pick_ref, four_ref
):
    c = lax.axis_index("c")

    @pl.when(c == 0)
    def _():
        set_up(factor_ref, top_ref, low_ref, pick_ref, four_ref)
        for j in range(4):
            field = field_ref[16 * j : 16 * j + 16].reshape(1024, 128)
            own = lax.dot_general(
                rows_for(0, factor_y_ref), field, (((1,), (1,)), ((), ())), precision=HIGHEST, preferred_element_type=F32
            )
            out_ref[j] = own + received_ref[j]

    @pl.when(c == 1)
    def _():
        out_ref[...] = mine_ref[...] + received_ref[...]


def add(field, factor_y, factor_z, received, early):
    return pl.pallas_call(
        add_kernel,
        out_shape=[HALF, FOUR, FOUR, PICK],
        scratch_shapes=[pltpu.VMEM((256, 384), F32)],
        input_output_aliases={5: 1, 6: 2, 7: 3},
        compiler_params=PARAMS,
    )(field, factor_y, factor_z, received, *early)


def z_kernel(parts_ref, factor_ref, rest_ref, out_ref):
    rows = []
    for t in range(4):
        lanes = slice(256 * t, 256 * t + 256)
        rows.append((parts_ref[0, :, lanes] + parts_ref[1, :, lanes]) + (parts_ref[2, :, lanes] + parts_ref[3, :, lanes]))
    top, low = split(jnp.concatenate(rows, axis=0))
    both = jnp.dot(jnp.concatenate([top, low], axis=0), factor_ref[...], preferred_element_type=F32)
    both = both[0:192] + both[192:384] + jnp.dot(top, rest_ref[...], preferred_element_type=F32)
    for t in range(4):
        for k in range(3):
            out_ref[pl.ds(4 * k + t, 48, stride=12), :] = both[48 * t : 48 * t + 48, 128 * k : 128 * k + 128]


def z_product(parts, factor, rest):
    return pl.pallas_call(
        z_kernel, out_shape=jax.ShapeDtypeStruct((576, 128), F32), compiler_params=PARAMS
    )(parts, factor, rest)


def copies_kernel(parts_ref, out_ref, both_ref):
    for h in range(2):
        both_ref[:, 4 * h : 4 * h + 4] = parts_ref[:, h].sum(0)
    for n in range(16):
        out_ref[n] = both_ref[...]


def copies(parts):
    return pl.pallas_call(
        copies_kernel,
        out_shape=jax.ShapeDtypeStruct((16, 9, 8, 128), F32),
        scratch_shapes=[pltpu.VMEM((9, 8, 128), F32)],
        compiler_params=PARAMS,
    )(parts)


def gram_kernel(both_ref, out_ref, terms_ref):
    x, y = lax.axis_index("x"), lax.axis_index("y")

    def rows_of(start, count, i):
        tiles = [both_ref[pl.ds(start, count), 3 * i + k].reshape(8 * count, 128) for k in range(3)]
        wide = jnp.concatenate(tiles, axis=1)
        return split(jnp.concatenate([wide[:, R * q : R * q + R] for q in range(4)], axis=0))

    total = jnp.zeros((256, 128), F32)
    for i in range(3):
        top, low = rows_of(8 * (x % 2), 8, i)
        right, rest = rows_of(4 * y, 4, i)
        total += dot_nt(top, right) + (dot_nt(low, right) + dot_nt(top, rest))
    terms_ref[0:256] = total
    first = (lax.broadcasted_iota(jnp.int32, (4, 128), 1) & 4) == 0
    for c in range(2):
        for k in range(4):
            for t in range(0, 4, 2):
                start = 32 * c + 8 * k + t + 4 * (x // 2)
                even = terms_ref[pl.ds(start, 4, stride=64), :]
                odd = terms_ref[pl.ds(start + 1, 4, stride=64), :]
                out_ref[2 * k + t // 2, c, 0] = jnp.where(first, even, pltpu.roll(odd, 4, 1))
                out_ref[2 * k + t // 2, c, 1] = jnp.where(first, pltpu.roll(even, 124, 1), odd)


def gram_terms(both):
    return pl.pallas_call(
        gram_kernel,
        out_shape=jax.ShapeDtypeStruct((8, 2, 2, 4, 128), F32),
        scratch_shapes=[pltpu.VMEM((320, 128), F32)],
        compiler_params=PARAMS,
    )(both)


def last_kernel(terms_ref, pick_ref, out_ref):
    total = terms_ref[...].sum(0)
    moved = lax.dot_general(
        total, pick_ref[...], (((1,), (1,)), ((), ())), precision=HIGHEST, preferred_element_type=F32
    ) / (R * R)
    out_ref[0:4] = moved[:, 0:64]
    out_ref[4:8] = moved[:, 64:128]


def last(terms, pick):
    return pl.pallas_call(
        last_kernel, out_shape=jax.ShapeDtypeStruct((8, 64), F32), compiler_params=PARAMS
    )(terms, pick).T


def body(species, factor_y, factor_z):
    others, field, factor_y = others_product(species, factor_y)
    early = early_product(field, factor_y, factor_z)
    along_y, factor, rest, pick = add(
        field, factor_y, factor_z, lax.ppermute(others, "c", [(0, 1), (1, 0)]), early
    )
    parts = z_product(lax.all_to_all(along_y, "x", 0, 0, tiled=True), factor, rest)
    parts = lax.all_to_all(parts.reshape(144, 4, 128), ("g", "h"), 0, 0, tiled=True)
    both = copies(parts.reshape(8, 2, 9, 4, 128)).reshape(144, 8, 128)
    both = lax.all_to_all(both, ("y", "x"), 0, 0, tiled=True)
    terms = gram_terms(both.reshape(16, 9, 8, 128)).reshape(32, 4, 128)
    return last(lax.all_to_all(terms, ("g", "c", "h"), 0, 0, tiled=True), pick)


def solution(mesh):
    fine = Mesh(mesh.devices.reshape(2, 4, 4, 2, 8), ("h", "y", "x", "c", "g"))
    placed = (P(("h", "y"), "g", ("x", "c")), P(("x", "c"), None), P("g", None))
    return jax.shard_map(
        body, mesh=fine, in_specs=placed, out_specs=P(("h", "y"), ("x", "c", "g")), check_vma=False
    )
```

```python
import jax
import jax.numpy as jnp
from jax import lax
from jax.experimental import pallas as pl
from jax.experimental.pallas import tpu as pltpu
from jax.sharding import Mesh, PartitionSpec as P

R = 96
HIGHEST = lax.Precision.HIGHEST
F32 = jnp.float32
BF16 = jnp.bfloat16
PARAMS = pltpu.CompilerParams(vmem_limit_bytes=32 * 1024 * 1024)


def split(value):
    top = value.astype(BF16)
    return top, (value - top.astype(F32)).astype(BF16)


def dot_nt(left, right):
    return lax.dot_general(left, right, (((1,), (1,)), ((), ())), preferred_element_type=F32)


def halves(rows):
    top, low = split(rows)
    upper = jnp.concatenate([top, top], axis=1)
    return jnp.concatenate([upper, jnp.concatenate([low, jnp.zeros_like(low)], axis=1)], axis=0)


def product(left, field):
    top, low = split(field.reshape(-1, 128))
    both = dot_nt(left, jnp.concatenate([top, low], axis=1))
    return both[0:48] + both[48:96]


def rows_for(core, factor_ref):
    return factor_ref[pl.ds(pl.multiple_of(48 * core, 48), 48)]


def others_kernel(species_hbm, factor_hbm, others_ref, field_ref, factor_ref, sems):
    copies = [pltpu.make_async_copy(factor_hbm, factor_ref, sems.at[2])]
    for j in range(2):
        rows = pl.ds(32 * j, 32)
        copies.append(pltpu.make_async_copy(species_hbm.at[rows], field_ref.at[rows], sems.at[j]))
    for copy in copies:
        copy.start()
    copies[0].wait()
    left = halves(rows_for(1 - lax.axis_index("c"), factor_ref))
    for j in range(4):
        if j % 2 == 0:
            copies[1 + j // 2].wait()
        others_ref[j] = product(left, field_ref[16 * j : 16 * j + 16])


def others_product(species, factor_y):
    hbm = pl.BlockSpec(memory_space=pltpu.HBM)
    return pl.pallas_call(
        others_kernel,
        in_specs=[hbm, hbm],
        out_shape=[
            jax.ShapeDtypeStruct((4, 48, 1024), F32),
            pltpu.VMEM((64, 64, 128), F32),
            pltpu.VMEM((R, 128), F32),
        ],
        scratch_shapes=[pltpu.SemaphoreType.DMA((3,))],
        compiler_params=PARAMS,
    )(pltpu.with_memory_space_constraint(species, pltpu.HBM), pltpu.with_memory_space_constraint(factor_y.T, pltpu.HBM))


def set_up(factor_ref, top_ref, low_ref, pick_ref, four_ref):
    four_ref[...] = jnp.zeros_like(four_ref)
    for q in range(4):
        four_ref[64 * q : 64 * q + 64, R * q : R * q + R] = factor_ref[...]
    top_ref[...], low_ref[...] = split(four_ref[...])
    row = lax.broadcasted_iota(jnp.int32, (128, 128), 0)
    lane = lax.broadcasted_iota(jnp.int32, (128, 128), 1)
    source = (row & 3) * 32 + ((row >> 4) & 3) * 8 + (row >> 6) * 4 + ((row >> 2) & 3)
    pick_ref[...] = jnp.where(lane == source, 1.0, 0.0).astype(F32)


FOUR = pltpu.VMEM((256, 384), BF16)
PICK = pltpu.VMEM((128, 128), F32)
HALF = pltpu.VMEM((4, 48, 1024), F32)


def early_kernel(field_ref, factor_y_ref, factor_ref, out_ref, top_ref, low_ref, pick_ref, four_ref):
    @pl.when(lax.axis_index("c") == 1)
    def _():
        set_up(factor_ref, top_ref, low_ref, pick_ref, four_ref)
        left = halves(rows_for(1, factor_y_ref))
        for j in range(4):
            out_ref[j] = product(left, field_ref[16 * j : 16 * j + 16])


def early_product(field, factor_y, factor_z):
    return pl.pallas_call(
        early_kernel,
        out_shape=[HALF, FOUR, FOUR, PICK],
        scratch_shapes=[pltpu.VMEM((256, 384), F32)],
        compiler_params=PARAMS,
    )(field, factor_y, factor_z)


def add_kernel(
    field_ref, factor_y_ref, factor_ref, received_ref, mine_ref, top_in, low_in, pick_in, out_ref, top_ref, low_ref, pick_ref, four_ref
):
    c = lax.axis_index("c")

    @pl.when(c == 0)
    def _():
        set_up(factor_ref, top_ref, low_ref, pick_ref, four_ref)
        for j in range(4):
            field = field_ref[16 * j : 16 * j + 16].reshape(1024, 128)
            own = lax.dot_general(
                rows_for(0, factor_y_ref), field, (((1,), (1,)), ((), ())), precision=HIGHEST, preferred_element_type=F32
            )
            out_ref[j] = own + received_ref[j]

    @pl.when(c == 1)
    def _():
        out_ref[...] = mine_ref[...] + received_ref[...]


def add(field, factor_y, factor_z, received, early):
    return pl.pallas_call(
        add_kernel,
        out_shape=[HALF, FOUR, FOUR, PICK],
        scratch_shapes=[pltpu.VMEM((256, 384), F32)],
        input_output_aliases={5: 1, 6: 2, 7: 3},
        compiler_params=PARAMS,
    )(field, factor_y, factor_z, received, *early)


def z_kernel(parts_ref, factor_ref, rest_ref, out_ref):
    rows = []
    for t in range(4):
        lanes = slice(256 * t, 256 * t + 256)
        rows.append((parts_ref[0, :, lanes] + parts_ref[1, :, lanes]) + (parts_ref[2, :, lanes] + parts_ref[3, :, lanes]))
    top, low = split(jnp.concatenate(rows, axis=0))
    both = jnp.dot(jnp.concatenate([top, low], axis=0), factor_ref[...], preferred_element_type=F32)
    both = both[0:192] + both[192:384] + jnp.dot(top, rest_ref[...], preferred_element_type=F32)
    for t in range(4):
        for k in range(3):
            out_ref[pl.ds(4 * k + t, 48, stride=12), :] = both[48 * t : 48 * t + 48, 128 * k : 128 * k + 128]


def z_product(parts, factor, rest):
    return pl.pallas_call(
        z_kernel, out_shape=jax.ShapeDtypeStruct((576, 128), F32), compiler_params=PARAMS
    )(parts, factor, rest)


def copies_kernel(parts_ref, out_ref, both_ref):
    for h in range(2):
        both_ref[:, 4 * h : 4 * h + 4] = parts_ref[:, h].sum(0)
    for n in range(16):
        out_ref[n] = both_ref[...]


def copies(parts):
    return pl.pallas_call(
        copies_kernel,
        out_shape=jax.ShapeDtypeStruct((16, 9, 8, 128), F32),
        scratch_shapes=[pltpu.VMEM((9, 8, 128), F32)],
        compiler_params=PARAMS,
    )(parts)


def gram_kernel(both_ref, out_ref, terms_ref):
    x, y = lax.axis_index("x"), lax.axis_index("y")

    def rows_of(start, count, i):
        tiles = [both_ref[pl.ds(start, count), 3 * i + k].reshape(8 * count, 128) for k in range(3)]
        wide = jnp.concatenate(tiles, axis=1)
        return split(jnp.concatenate([wide[:, R * q : R * q + R] for q in range(4)], axis=0))

    total = jnp.zeros((256, 128), F32)
    for i in range(3):
        top, low = rows_of(8 * (x % 2), 8, i)
        right, rest = rows_of(4 * y, 4, i)
        total += dot_nt(top, right) + (dot_nt(low, right) + dot_nt(top, rest))
    terms_ref[0:256] = total
    first = (lax.broadcasted_iota(jnp.int32, (4, 128), 1) & 4) == 0
    for c in range(2):
        for k in range(4):
            for t in range(0, 4, 2):
                start = 32 * c + 8 * k + t + 4 * (x // 2)
                even = terms_ref[pl.ds(start, 4, stride=64), :]
                odd = terms_ref[pl.ds(start + 1, 4, stride=64), :]
                out_ref[0, c, 2 * k + t // 2] = jnp.where(first, even, pltpu.roll(odd, 4, 1))
                out_ref[1, c, 2 * k + t // 2] = jnp.where(first, pltpu.roll(even, 124, 1), odd)


def gram_terms(both):
    return pl.pallas_call(
        gram_kernel,
        out_shape=jax.ShapeDtypeStruct((2, 2, 8, 4, 128), F32),
        scratch_shapes=[pltpu.VMEM((320, 128), F32)],
        compiler_params=PARAMS,
    )(both)


def last_kernel(terms_ref, pick_ref, out_ref):
    total = terms_ref[...].sum(0)
    moved = lax.dot_general(
        total, pick_ref[...], (((1,), (1,)), ((), ())), precision=HIGHEST, preferred_element_type=F32
    ) / (R * R)
    out_ref[0:4] = moved[:, 0:64]
    out_ref[4:8] = moved[:, 64:128]


def last(terms, pick):
    return pl.pallas_call(
        last_kernel, out_shape=jax.ShapeDtypeStruct((8, 64), F32), compiler_params=PARAMS
    )(terms, pick).T


def body(species, factor_y, factor_z):
    others, field, factor_y = others_product(species, factor_y)
    early = early_product(field, factor_y, factor_z)
    along_y, factor, rest, pick = add(
        field, factor_y, factor_z, lax.ppermute(others, "c", [(0, 1), (1, 0)]), early
    )
    parts = z_product(lax.all_to_all(along_y, "x", 0, 0, tiled=True), factor, rest)
    parts = lax.all_to_all(parts.reshape(144, 4, 128), ("g", "h"), 0, 0, tiled=True)
    both = copies(parts.reshape(8, 2, 9, 4, 128)).reshape(144, 8, 128)
    both = lax.all_to_all(both, ("y", "x"), 0, 0, tiled=True)
    terms = gram_terms(both.reshape(16, 9, 8, 128)).reshape(32, 4, 128)
    return last(lax.all_to_all(terms, ("h", "c", "g"), 0, 0, tiled=True), pick)


def solution(mesh):
    fine = Mesh(mesh.devices.reshape(2, 4, 4, 2, 8), ("h", "y", "x", "c", "g"))
    placed = (P(("h", "y"), "g", ("x", "c")), P(("x", "c"), None), P("g", None))
    return jax.shard_map(
        body, mesh=fine, in_specs=placed, out_specs=P(("h", "y"), ("x", "c", "g")), check_vma=False
    )
```
